32 devices in a mesh: groups: 2 (over y), cols: 4 (over z), rows: 4 (over x, core).
Axes of the slice: x: 2, y: 2, z: 4, core: 2. Of those that a mesh axis runs over, the one named last changes fastest.
Arguments:
- acts: bfloat16 [4, 257, 1536], P('groups', None, 'rows'), parts along dimension 0, may hold values from -6 to 6
- out_grad: bfloat16 [4, 257, 1536], P('groups', None, 'rows'), parts along dimension 0, may hold values from -0.59765625 to 0.59765625
- w_in: bfloat16 [1536, 6144], P(None, 'cols'), may hold values from -0.15625 to 0.15625
- bias_in: bfloat16 [6144], P('cols'), may hold values from -4 to 4
- w_out: bfloat16 [6144, 1536], P('cols'), may hold values from -0.15625 to 0.15625
- sign_bits: int32 [16777216], P(('cols', 'rows')), may hold values 0 or 1
- picks: int32 [4096], replicated, may hold values from 0 to 16777215, as said below
Outputs:
- sketch: float32 [4, 4096], P('groups'), parts along dimension 0
The draws below stay inside these ranges and needn't reach their ends.
There are 2 independent parts, one for each index of `groups`. The reference program is written for one: setup_inputs(seed, part) draws one part's arguments, and reference() takes and returns one part's arrays. A program takes and returns all parts, laid end to end along the dimension named above; an argument that names none is the same for every part. Nothing has to cross between parts.
Inputs may be any that keep to these rules, and one draw needn't show every extreme that they name: `picks`: 4096 distinct positions in increasing order; the first is 0 and the last is 16777215.
All inputs are finite; a program needn't handle non-finite values. No bound on the sum of `sign_bits` on one device may be relied on, other than what follows from the above.
Results may differ from the reference program's by a relative error of at most 0.0031.
Values may be sent and summed in bfloat16 or wider, within the bound.
A program may use at most 192 MiB of HBM per device.

```python
import math
import jax
import jax.numpy as jnp
from jax import lax

D = 1536
F = 6144
TOK = 257
IMG = 2
SAMPLES = 4096
PAD = 16777216
COL_SHARDS = 4
ROW_SHARDS = 4
SHARDS = 16
LOCAL = 1048576
BLOCK_R = 384
BLOCK_C = 1536


def draw_picks(key, part):
    key = jax.random.fold_in(key, 7)
    middle_picks = jax.random.choice(key, PAD - 2, (SAMPLES - 2,), replace=False).astype(jnp.int32) + 1
    end_picks = jnp.array([0, PAD - 1], jnp.int32)
    return jnp.sort(jnp.concatenate([end_picks, middle_picks]))


def plant(result, rng, smallest, largest):
    dims = result.shape
    spot = [jax.random.randint(jax.random.fold_in(rng, axis), (), 0, dims[axis]) for axis in range(len(dims))]
    result = result.at[tuple(spot)].set(smallest)
    longest = dims.index(max(dims))
    spot[longest] = (spot[longest] + 1) % dims[longest]
    return result.at[tuple(spot)].set(largest)


def steps_of(key, extent, shards, low, top_value):
    loudness = 1.0
    for axis_at, blocks in shards:
        draws = jax.random.uniform(jax.random.fold_in(jax.random.fold_in(key, 6), axis_at), (blocks,), jnp.float32, low / len(shards), top_value / len(shards))
        loudness = loudness * jnp.repeat(jnp.exp(draws), extent[axis_at] // blocks).reshape((-1,) + (1,) * (len(extent) - 1 - axis_at))
    return loudness


def centred(stream_key, dims, width, most, split=(), held_as=jnp.bfloat16):
    values = jax.random.normal(stream_key, dims, jnp.float32) * width
    if len(split) > 0:
        values = steps_of(stream_key, dims, split, -0.22, 0.18) * values
    return jnp.clip(values, min=-most, max=most).astype(held_as)


def setup_inputs(seed: int = 0, part: int = 0) -> dict:
    keys = jax.random.split(jax.random.key(seed), 8)
    own_keys = jax.random.split(jax.random.fold_in(keys[7], part), 8)
    return {
        "acts": centred(own_keys[0], (IMG, TOK, D), 1.0, 6.0, ((2, 4),)),
        "out_grad": centred(own_keys[1], (IMG, TOK, D), 0.1, 0.59765625, ((2, 4),)),
        "w_in": centred(keys[2], (D, F), D ** -0.5, 0.15625, ((1, 4),)),
        "bias_in": centred(keys[3], (F,), 1.0, 4.0, ((0, 4),)),
        "w_out": centred(keys[4], (F, D), D ** -0.5, 0.15625, ((0, 4),)),
        "sign_bits": plant((jax.random.randint(keys[5], (PAD,), 0, 2) < 1).astype(jnp.int32), jax.random.fold_in(keys[5], 1), 0, 1),
        "picks": draw_picks(jax.random.fold_in(keys[7], 71), part),
    }


root_half = 0.7071067811865476
inv_root_two_pi = 0.3989422804014327

def gelu_slope(inputs):
    normal_cdf = 0.5 * (1.0 + jax.scipy.special.erf(inputs * root_half))
    return normal_cdf + inputs * inv_root_two_pi * jnp.exp(-0.5 * inputs * inputs)

def sign_table(order_len):
    row_ids = jnp.arange(order_len, dtype=jnp.int32)[:, None]
    col_ids = jnp.arange(order_len, dtype=jnp.int32)[None, :]
    shared = jnp.bitwise_and(row_ids, col_ids)
    parity = jnp.zeros((order_len, order_len), jnp.int32)
    for bit_pos in range(order_len.bit_length() - 1):
        parity = jnp.bitwise_xor(parity, jnp.bitwise_and(jnp.right_shift(shared, bit_pos), 1))
    return (1 - 2 * parity).astype(jnp.float32)

def apply_factor(signal, lead_size, finished, factor_len, length):
    matrix = sign_table(factor_len)
    remain = length // (finished * factor_len)
    if remain == 1:
        flat_rows = signal.reshape(lead_size * finished, factor_len)
        signal = jnp.dot(flat_rows, matrix, precision=lax.Precision.HIGHEST, preferred_element_type=jnp.float32)
    else:
        grouped = signal.reshape(lead_size * finished, factor_len, remain)
        signal = jnp.einsum('fg,pfq->pgq', matrix, grouped, precision=lax.Precision.HIGHEST, preferred_element_type=jnp.float32)
    return signal.reshape(lead_size, length)

def transform(signal):
    lead_size = signal.shape[0]
    length = signal.shape[1]
    levels = length.bit_length() - 1
    full_count, low_bits = divmod(levels, 7)
    finished = 1
    if low_bits > 0:
        signal = apply_factor(signal, lead_size, 1, 2 ** low_bits, length)
        finished = 2 ** low_bits
    for section_pos in range(full_count):
        signal = apply_factor(signal, lead_size, finished, 128, length)
        finished = finished * 128
    return signal

def reference(acts, out_grad, w_in, bias_in, w_out, sign_bits, picks):
    sign_values = (1 - 2 * sign_bits).astype(jnp.float32)

    def one_image(image_pair):
        act_img, grad_img = image_pair
        pre_act = jnp.dot(act_img, w_in, preferred_element_type=jnp.float32) + bias_in.astype(jnp.float32)[None, :]
        post_grad = lax.dot_general(grad_img, w_out, (((1,), (1,)), ((), ())), preferred_element_type=jnp.float32)
        pre_grad = (post_grad * gelu_slope(pre_act)).astype(jnp.bfloat16)
        weight_grad = jnp.dot(act_img.T, pre_grad, preferred_element_type=jnp.float32)
        tile_rows = weight_grad.reshape(ROW_SHARDS, BLOCK_R, COL_SHARDS, BLOCK_C).transpose(2, 0, 1, 3)
        tile_rows = tile_rows.reshape(SHARDS, BLOCK_R * BLOCK_C)
        padded = jnp.pad(tile_rows, ((0, 0), (0, LOCAL - BLOCK_R * BLOCK_C))).reshape(1, PAD)
        mixed_all = transform(padded * sign_values[None, :])
        return jnp.take(mixed_all[0], picks) * (1.0 / math.sqrt(PAD))
    return lax.map(one_image, (acts, out_grad))
```

```python
import functools
import math

import jax
import jax.numpy as jnp
from jax import lax
from jax.experimental import pallas as pl
from jax.experimental.pallas import tpu as pltpu
from jax.sharding import PartitionSpec as P

root_half = 0.7071067811865476
inv_root_two_pi = 0.3989422804014327
LANES = 128
MESH = pl.DeviceIdType.MESH


def gelu_slope(inputs):
    normal_cdf = 0.5 * (1.0 + lax.erf(inputs * root_half))
    return normal_cdf + inputs * inv_root_two_pi * jnp.exp(-0.5 * inputs * inputs)


def signs_of(left, right):
    odd = jnp.bitwise_and(lax.population_count(jnp.bitwise_and(left, right)), 1)
    return (1 - 2 * odd).astype(jnp.float32)


def low_part(hidden_part):
    return hidden_part & -hidden_part


def plain_body(acts, out_grad, w_in, bias_in, w_out, sign_bits, picks):
    images, tokens, width_part = acts.shape
    hidden_part = w_in.shape[1]
    low_len = low_part(hidden_part)
    act_all = lax.all_gather(acts, "rows", axis=2, tiled=True)
    grad_all = lax.all_gather(out_grad, "rows", axis=2, tiled=True)
    pre_act = jnp.einsum("itd,df->itf", act_all, w_in, preferred_element_type=jnp.float32)
    pre_act = pre_act + bias_in.astype(jnp.float32)
    back = jnp.einsum("itd,fd->itf", grad_all, w_out, preferred_element_type=jnp.float32)
    pre_grad = (back * gelu_slope(pre_act)).astype(jnp.bfloat16)
    weight_grad = jnp.einsum("itd,itf->idf", acts, pre_grad, preferred_element_type=jnp.float32)
    local_len = sign_bits.shape[0]
    used = width_part * hidden_part
    flips = (1 - 2 * sign_bits[:used]).astype(jnp.float32)
    signed = (weight_grad.reshape(images, used) * flips).astype(jnp.bfloat16)
    signed = signed.reshape(images, used // low_len, low_len)
    inside = picks % local_len
    high_signs = signs_of((inside // low_len)[:, None], jnp.arange(used // low_len)[None, :])
    low_signs = signs_of((inside % low_len)[:, None], jnp.arange(low_len)[None, :])
    half = jnp.einsum(
        "mq,iql->iml", high_signs.astype(jnp.bfloat16), signed, preferred_element_type=jnp.float32
    )
    shards = lax.axis_size(("cols", "rows"))
    me = lax.axis_index(("cols", "rows"))
    contrib = jnp.sum(half * low_signs[None], axis=2) * signs_of(picks // local_len, me)[None, :]
    return lax.psum(contrib, ("cols", "rows")) * (1.0 / math.sqrt(local_len * shards))


def kernel(
    local_len,
    blocks_hbm,
    w_in_hbm,
    bias_ref,
    w_out_hbm,
    bits_hbm,
    picks_ref,
    out_ref,
    blocks,
    w_in,
    w_out,
    bits,
    high,
    low,
    signed,
    sems,
):
    row_shards, _, tokens, width = blocks.shape
    hidden = w_in.shape[1]
    low_len = low.shape[1]
    groups = hidden // low_len
    images = out_ref.shape[0]
    image_rows = tokens // images
    me_row = lax.axis_index("rows")
    me_all = lax.axis_index("cols") * lax.axis_size("rows") + me_row
    copies = [
        pltpu.make_async_copy(blocks_hbm, blocks, sems.at[0]),
        pltpu.make_async_copy(w_in_hbm, w_in, sems.at[1]),
        pltpu.make_async_copy(w_out_hbm, w_out, sems.at[2]),
        pltpu.make_async_copy(bits_hbm.at[pl.ds(0, bits.shape[0])], bits, sems.at[3]),
    ]
    for copy in copies:
        copy.start()

    lane = lax.broadcasted_iota(jnp.int32, (LANES, LANES), 1)

    def make_signs(at, _):
        column = jnp.broadcast_to(picks_ref[pl.ds(at, 1), :], (LANES, LANES)).T
        inside = jnp.bitwise_and(column, local_len - 1)
        upper = jnp.right_shift(inside, low_len.bit_length() - 1)
        lower = jnp.bitwise_and(inside, low_len - 1)
        rows = pl.ds(pl.multiple_of(at * LANES, LANES), LANES)
        for group in range(groups):
            for tile in range(width // LANES):
                place = groups * (lane + tile * LANES) + group
                start = group * width + tile * LANES
                high[rows, start : start + LANES] = signs_of(upper, place).astype(jnp.bfloat16)
        for tile in range(low_len // LANES):
            low[rows, tile * LANES : (tile + 1) * LANES] = signs_of(
                lower, lane + tile * LANES
            ).astype(jnp.bfloat16)
        return 0

    lax.fori_loop(0, picks_ref.shape[0], make_signs, 0)
    for copy in copies:
        copy.wait()

    for group in range(groups):
        cols = slice(group * low_len, (group + 1) * low_len)
        pre = jnp.broadcast_to(bias_ref[:, cols].astype(jnp.float32), (tokens, low_len))
        back = jnp.zeros((tokens, low_len), jnp.float32)
        for row in range(row_shards):
            part = slice(row * width, (row + 1) * width)
            pre = pre + jnp.dot(
                blocks[row, 0], w_in[part, cols], preferred_element_type=jnp.float32
            )
            back = back + lax.dot_general(
                blocks[row, 1],
                w_out[cols, part],
                (((1,), (1,)), ((), ())),
                preferred_element_type=jnp.float32,
            )
        pre_grad = (back * gelu_slope(pre)).astype(jnp.bfloat16)
        for image in range(images):
            rows = slice(image * image_rows, (image + 1) * image_rows)
            grad = lax.dot_general(
                blocks[me_row, 0, rows, :],
                pre_grad[rows],
                (((0,), (0,)), ((), ())),
                preferred_element_type=jnp.float32,
            )
            for tile in range(low_len // LANES):
                first = group * (low_len // LANES) + tile
                flips = bits[pl.ds(first, width, stride=hidden // LANES), :]
                piece = grad[:, tile * LANES : (tile + 1) * LANES]
                start = image * low_len + tile * LANES
                signed[group * width : (group + 1) * width, start : start + LANES] = (
                    piece * (1 - 2 * flips).astype(jnp.float32)
                ).astype(jnp.bfloat16)

    scale = 1.0 / math.sqrt(local_len * lax.axis_size("cols") * row_shards)
    step = 2 * LANES

    def select(at, _):
        rows = pl.ds(pl.multiple_of(at * step, step), step)
        half = jnp.dot(high[rows, :], signed[...], preferred_element_type=jnp.float32)
        weight = low[rows, :].astype(jnp.float32)
        for image in range(images):
            total = jnp.zeros((step, LANES), jnp.float32)
            for tile in range(low_len // LANES):
                start = image * low_len + tile * LANES
                total = total + half[:, start : start + LANES] * weight[
                    :, tile * LANES : (tile + 1) * LANES
                ]
            for part in range(2):
                block = total[part * LANES : (part + 1) * LANES].T
                out_ref[image, pl.ds(2 * at + part, 1), :] = jnp.sum(block, axis=0, keepdims=True)
        return 0

    lax.fori_loop(0, picks_ref.shape[0] // 2, select, 0)
    owner = jnp.right_shift(picks_ref[...], local_len.bit_length() - 1)
    facing = signs_of(owner, jnp.broadcast_to(me_all, owner.shape)) * scale
    for image in range(images):
        out_ref[image] = out_ref[image] * facing


def body(acts, out_grad, w_in, bias_in, w_out, sign_bits, picks):
    images, tokens, width = acts.shape
    hidden = w_in.shape[1]
    low_len = low_part(hidden)
    if low_len % LANES or width % LANES or picks.shape[0] % (16 * LANES):
        return plain_body(acts, out_grad, w_in, bias_in, w_out, sign_bits, picks)
    row_shards = lax.axis_size("rows")
    local_len = sign_bits.shape[0]
    padded = -(-tokens // 16) * 16
    own = jnp.pad(jnp.stack([acts, out_grad]), ((0, 0), (0, 0), (0, padded - tokens), (0, 0)))
    own = own.reshape(2, images * padded, width)
    blocks = lax.all_gather(own, "rows", axis=0, tiled=False)
    groups = hidden // low_len
    count = picks.shape[0]
    contrib = pl.pallas_call(
        functools.partial(kernel, local_len),
        out_shape=jax.ShapeDtypeStruct((images, count // LANES, LANES), jnp.float32),
        in_specs=[
            pl.BlockSpec(memory_space=pl.ANY),
            pl.BlockSpec(memory_space=pl.ANY),
            pl.BlockSpec(memory_space=pltpu.VMEM),
            pl.BlockSpec(memory_space=pl.ANY),
            pl.BlockSpec(memory_space=pl.ANY),
            pl.BlockSpec(memory_space=pltpu.VMEM),
        ],
        out_specs=pl.BlockSpec(memory_space=pltpu.VMEM),
        scratch_shapes=[
            pltpu.VMEM((row_shards, 2, images * padded, width), jnp.bfloat16),
            pltpu.VMEM(w_in.shape, jnp.bfloat16),
            pltpu.VMEM(w_out.shape, jnp.bfloat16),
            pltpu.VMEM((width * hidden // LANES, LANES), jnp.int32),
            pltpu.VMEM((count, groups * width), jnp.bfloat16),
            pltpu.VMEM((count, low_len), jnp.bfloat16),
            pltpu.VMEM((groups * width, images * low_len), jnp.bfloat16),
            pltpu.SemaphoreType.DMA((4,)),
        ],
        compiler_params=pltpu.CompilerParams(vmem_limit_bytes=56 * 2**20),
    )(
        blocks,
        w_in,
        bias_in.reshape(1, hidden),
        w_out,
        sign_bits.reshape(local_len // LANES, LANES),
        picks.reshape(count // LANES, LANES),
    )
    return lax.psum(contrib, ("cols", "rows")).reshape(images, count)


def solution(mesh):
    return jax.shard_map(
        body,
        mesh=mesh,
        in_specs=(
            P("groups", None, "rows"),
            P("groups", None, "rows"),
            P(None, "cols"),
            P("cols"),
            P("cols", None),
            P(("cols", "rows")),
            P(),
        ),
        out_specs=P("groups", None),
        check_vma=False,
    )
```

```python
import functools
import math

import jax
import jax.numpy as jnp
from jax import lax
from jax.experimental import pallas as pl
from jax.experimental.pallas import tpu as pltpu
from jax.sharding import PartitionSpec as P

root_half = 0.7071067811865476
inv_root_two_pi = 0.3989422804014327
LANES = 128
MESH = pl.DeviceIdType.MESH


def gelu_slope(inputs):
    normal_cdf = 0.5 * (1.0 + lax.erf(inputs * root_half))
    return normal_cdf + inputs * inv_root_two_pi * jnp.exp(-0.5 * inputs * inputs)


def signs_of(left, right):
    odd = jnp.bitwise_and(lax.population_count(jnp.bitwise_and(left, right)), 1)
    return (1 - 2 * odd).astype(jnp.float32)


def low_part(hidden_part):
    return hidden_part & -hidden_part


def plain_body(acts, out_grad, w_in, bias_in, w_out, sign_bits, picks):
    images, tokens, width_part = acts.shape
    hidden_part = w_in.shape[1]
    low_len = low_part(hidden_part)
    act_all = lax.all_gather(acts, "rows", axis=2, tiled=True)
    grad_all = lax.all_gather(out_grad, "rows", axis=2, tiled=True)
    pre_act = jnp.einsum("itd,df->itf", act_all, w_in, preferred_element_type=jnp.float32)
    pre_act = pre_act + bias_in.astype(jnp.float32)
    back = jnp.einsum("itd,fd->itf", grad_all, w_out, preferred_element_type=jnp.float32)
    pre_grad = (back * gelu_slope(pre_act)).astype(jnp.bfloat16)
    weight_grad = jnp.einsum("itd,itf->idf", acts, pre_grad, preferred_element_type=jnp.float32)
    local_len = sign_bits.shape[0]
    used = width_part * hidden_part
    flips = (1 - 2 * sign_bits[:used]).astype(jnp.float32)
    signed = (weight_grad.reshape(images, used) * flips).astype(jnp.bfloat16)
    signed = signed.reshape(images, used // low_len, low_len)
    inside = picks % local_len
    high_signs = signs_of((inside // low_len)[:, None], jnp.arange(used // low_len)[None, :])
    low_signs = signs_of((inside % low_len)[:, None], jnp.arange(low_len)[None, :])
    half = jnp.einsum(
        "mq,iql->iml", high_signs.astype(jnp.bfloat16), signed, preferred_element_type=jnp.float32
    )
    shards = lax.axis_size(("cols", "rows"))
    me = lax.axis_index(("cols", "rows"))
    contrib = jnp.sum(half * low_signs[None], axis=2) * signs_of(picks // local_len, me)[None, :]
    return lax.psum(contrib, ("cols", "rows")) * (1.0 / math.sqrt(local_len * shards))


def kernel(
    local_len,
    col_shards,
    acts_ref,
    grads_ref,
    w_in_hbm,
    bias_ref,
    w_out_hbm,
    bits_hbm,
    picks_ref,
    out_ref,
    blocks,
    w_in,
    w_out,
    bits,
    high,
    low,
    signed,
    pre_sum,
    back_sum,
    mixed,
    incoming,
    load_sems,
    twin_sems,
    far_sems,
    layer_sems,
    pass_far_sems,
    pass_layer_sems,
    sum_sems,
):
    images, tokens, width = acts_ref.shape
    image_rows = blocks.shape[1] // images
    hidden = w_in.shape[1]
    low_len = low.shape[1]
    groups = hidden // low_len
    row_shards = 4
    row = lax.axis_index("rows")
    col = lax.axis_index("cols")
    me_all = col * row_shards + row

    twin = row + 1 - 2 * lax.rem(row, 2)
    far = lax.rem(row + 2, row_shards)
    partners = [{"rows": twin}, {"rows": far}]
    hop = 1
    while hop < col_shards:
        partners.append({"cols": col + hop - 2 * hop * lax.rem(col // hop, 2)})
        hop *= 2
    layer = partners[2]

    barrier = pltpu.get_barrier_semaphore()
    for partner in partners:
        pl.semaphore_signal(barrier, inc=1, device_id=partner, device_id_type=MESH)

    loads = [
        pltpu.make_async_copy(bits_hbm.at[pl.ds(0, bits.shape[0])], bits, load_sems.at[0]),
        pltpu.make_async_copy(w_in_hbm, w_in, load_sems.at[1]),
        pltpu.make_async_copy(w_out_hbm, w_out, load_sems.at[2]),
    ]
    for load in loads[1:] + loads[:1]:
        load.start()

    own_cols = pl.ds(pl.multiple_of(row * width, LANES), width)
    gap = jnp.zeros((image_rows - tokens, width), jnp.bfloat16)
    for image in range(images):
        for kind, ref in enumerate((acts_ref, grads_ref)):
            blocks[kind, image * image_rows : (image + 1) * image_rows, own_cols] = (
                jnp.concatenate([ref[image], gap], axis=0)
            )
    pl.semaphore_wait(barrier, len(partners))

    tiles = images * image_rows // 16
    count = far_sems.shape[1]
    edges = [16 * (tiles * part // count) for part in range(count + 1)]

    def place(kind, owner, part):
        rows = pl.ds(0, images * image_rows)
        if part is not None:
            rows = pl.ds(edges[part], edges[part + 1] - edges[part])
        return blocks.at[kind, rows, pl.ds(pl.multiple_of(owner * width, LANES), width)]

    def send(ref, sems, at, partner):
        return pltpu.make_async_remote_copy(
            src_ref=ref,
            dst_ref=ref,
            send_sem=sems.at[0, at],
            recv_sem=sems.at[1, at],
            device_id=partner,
            device_id_type=MESH,
        )

    mine = lax.rem(col, 2)
    to_far = [send(place(mine, row, part), far_sems, part, partners[1]) for part in range(count)]
    to_twin = [send(place(kind, row, None), twin_sems, kind, partners[0]) for kind in range(2)]
    to_layer = [send(place(mine, far, part), layer_sems, part, layer) for part in range(count)]
    pass_far = [
        send(place(mine, far, part), pass_far_sems, part, partners[0]) for part in range(count)
    ]
    pass_layer = [
        send(place(1 - mine, far, part), pass_layer_sems, part, partners[0])
        for part in range(count)
    ]
    for copy in to_far + to_twin:
        copy.start()

    def relay_far(part):
        to_far[part].wait_recv()
        to_layer[part].start()
        pass_far[part].start()

    def relay_layer(part):
        to_layer[part].wait_recv()
        pass_layer[part].start()

    lane = lax.broadcasted_iota(jnp.int32, (LANES, LANES), 1)

    def make_signs(at, _):
        column = jnp.broadcast_to(picks_ref[pl.ds(at, 1), :], (LANES, LANES)).T
        inside = jnp.bitwise_and(column, local_len - 1)
        upper = jnp.right_shift(inside, low_len.bit_length() - 1)
        lower = jnp.bitwise_and(inside, low_len - 1)
        rows = pl.ds(pl.multiple_of(at * LANES, LANES), LANES)
        for group in range(groups):
            for tile in range(width // LANES):
                spot = groups * (lane + tile * LANES) + group
                start = group * width + tile * LANES
                high[rows, start : start + LANES] = signs_of(upper, spot).astype(jnp.bfloat16)
        for tile in range(low_len // LANES):
            low[rows, tile * LANES : (tile + 1) * LANES] = signs_of(
                lower, lane + tile * LANES
            ).astype(jnp.bfloat16)
        return 0

    def signs(part):
        every = picks_ref.shape[0]
        lax.fori_loop(every * part // 4, every * (part + 1) // 4, make_signs, 0)

    pair = 2 * width

    def products(half, group):
        cols = slice(group * low_len, (group + 1) * low_len)
        part = pl.ds(pl.multiple_of(half * pair, LANES), pair)
        pre = jnp.dot(blocks[0, :, part], w_in[part, cols], preferred_element_type=jnp.float32)
        back = lax.dot_general(
            blocks[1, :, part],
            w_out[cols, part],
            (((1,), (1,)), ((), ())),
            preferred_element_type=jnp.float32,
        )
        return pre, back

    here = row // 2

    def own_products(group):
        cols = slice(group * low_len, (group + 1) * low_len)
        pre, back = products(here, group)
        pre_sum[:, cols] = pre + bias_ref[:, cols].astype(jnp.float32)
        back_sum[:, cols] = back

    signs(0)
    signs(1)
    relay_far(0)
    signs(2)
    relay_far(1)
    signs(3)
    relay_layer(0)
    relay_far(2)
    for load in loads[1:]:
        load.wait()
    for copy in to_twin:
        copy.wait_recv()
    own_products(0)
    relay_far(3)
    relay_layer(1)
    for group in range(1, groups):
        own_products(group)
    relay_layer(2)
    relay_layer(3)
    loads[0].wait()
    for copy in pass_far + pass_layer:
        copy.wait_recv()

    for group in range(groups):
        cols = slice(group * low_len, (group + 1) * low_len)
        pre, back = products(1 - here, group)
        pre = pre + pre_sum[:, cols]
        back = back + back_sum[:, cols]
        pre_grad = (back * gelu_slope(pre)).astype(jnp.bfloat16)
        for image in range(images):
            rows = slice(image * image_rows, (image + 1) * image_rows)
            grad = lax.dot_general(
                blocks[0, rows, own_cols],
                pre_grad[rows],
                (((0,), (0,)), ((), ())),
                preferred_element_type=jnp.float32,
            )
            for tile in range(low_len // LANES):
                first = group * (low_len // LANES) + tile
                flips = bits[pl.ds(first, width, stride=hidden // LANES), :]
                piece = grad[:, tile * LANES : (tile + 1) * LANES]
                start = image * low_len + tile * LANES
                signed[group * width : (group + 1) * width, start : start + LANES] = (
                    piece * (1 - 2 * flips).astype(jnp.float32)
                ).astype(jnp.bfloat16)

    step = 2 * LANES

    def select(at, _):
        rows = pl.ds(pl.multiple_of(at * step, step), step)
        half = jnp.dot(high[rows, :], signed[...], preferred_element_type=jnp.float32)
        weight = low[rows, :].astype(jnp.float32)
        for image in range(images):
            total = jnp.zeros((step, LANES), jnp.float32)
            for tile in range(low_len // LANES):
                start = image * low_len + tile * LANES
                total = total + half[:, start : start + LANES] * weight[
                    :, tile * LANES : (tile + 1) * LANES
                ]
            for part in range(2):
                block = total[part * LANES : (part + 1) * LANES].T
                mixed[image, pl.ds(2 * at + part, 1), :] = jnp.sum(block, axis=0, keepdims=True)
        return 0

    lax.fori_loop(0, picks_ref.shape[0] // 2, select, 0)
    scale = 1.0 / math.sqrt(local_len * col_shards * row_shards)
    owner = jnp.right_shift(picks_ref[...], local_len.bit_length() - 1)
    facing = signs_of(owner, jnp.broadcast_to(me_all, owner.shape)) * scale
    for image in range(images):
        mixed[image] = mixed[image] * facing

    for at, partner in enumerate(partners):
        copy = pltpu.make_async_remote_copy(
            src_ref=mixed,
            dst_ref=incoming.at[at],
            send_sem=sum_sems.at[0, at],
            recv_sem=sum_sems.at[1, at],
            device_id=partner,
            device_id_type=MESH,
        )
        copy.start()
        copy.wait()
        if at < len(partners) - 1:
            mixed[...] = mixed[...] + incoming[at]
        else:
            out_ref[...] = mixed[...] + incoming[at]
    for copy in to_far + to_twin + to_layer + pass_far + pass_layer:
        copy.wait_send()


def body(acts, out_grad, w_in, bias_in, w_out, sign_bits, picks):
    images, tokens, width = acts.shape
    hidden = w_in.shape[1]
    low_len = low_part(hidden)
    row_shards = lax.axis_size("rows")
    col_shards = lax.axis_size("cols")
    fits = low_len % LANES == 0 and width % LANES == 0 and picks.shape[0] % (16 * LANES) == 0
    if not fits or row_shards != 4 or col_shards < 2 or col_shards & (col_shards - 1):
        return plain_body(acts, out_grad, w_in, bias_in, w_out, sign_bits, picks)
    local_len = sign_bits.shape[0]
    padded = -(-tokens // 16) * 16
    groups = hidden // low_len
    count = picks.shape[0]
    parts = 4
    steps = 1 + col_shards.bit_length()
    sketch_shape = (images, count // LANES, LANES)
    vmem = pl.BlockSpec(memory_space=pltpu.VMEM)
    anywhere = pl.BlockSpec(memory_space=pl.ANY)
    sketch = pl.pallas_call(
        functools.partial(kernel, local_len, col_shards),
        out_shape=jax.ShapeDtypeStruct(sketch_shape, jnp.float32),
        in_specs=[vmem, vmem, anywhere, vmem, anywhere, anywhere, vmem],
        out_specs=vmem,
        scratch_shapes=[
            pltpu.VMEM((2, images * padded, row_shards * width), jnp.bfloat16),
            pltpu.VMEM(w_in.shape, jnp.bfloat16),
            pltpu.VMEM(w_out.shape, jnp.bfloat16),
            pltpu.VMEM((width * hidden // LANES, LANES), jnp.int32),
            pltpu.VMEM((count, groups * width), jnp.bfloat16),
            pltpu.VMEM((count, low_len), jnp.bfloat16),
            pltpu.VMEM((groups * width, images * low_len), jnp.bfloat16),
            pltpu.VMEM((images * padded, hidden), jnp.float32),
            pltpu.VMEM((images * padded, hidden), jnp.float32),
            pltpu.VMEM(sketch_shape, jnp.float32),
            pltpu.VMEM((steps,) + sketch_shape, jnp.float32),
            pltpu.SemaphoreType.DMA((3,)),
            pltpu.SemaphoreType.DMA((2, 2)),
            pltpu.SemaphoreType.DMA((2, parts)),
            pltpu.SemaphoreType.DMA((2, parts)),
            pltpu.SemaphoreType.DMA((2, parts)),
            pltpu.SemaphoreType.DMA((2, parts)),
            pltpu.SemaphoreType.DMA((2, steps)),
        ],
        compiler_params=pltpu.CompilerParams(
            vmem_limit_bytes=56 * 2**20, collective_id=0, has_side_effects=True
        ),
    )(
        acts,
        out_grad,
        w_in,
        bias_in.reshape(1, hidden),
        w_out,
        sign_bits.reshape(local_len // LANES, LANES),
        picks.reshape(count // LANES, LANES),
    )
    return sketch.reshape(images, count)


def solution(mesh):
    return jax.shard_map(
        body,
        mesh=mesh,
        in_specs=(
            P("groups", None, "rows"),
            P("groups", None, "rows"),
            P(None, "cols"),
            P("cols"),
            P("cols", None),
            P(("cols", "rows")),
            P(),
        ),
        out_specs=P("groups", None),
        check_vma=False,
    )
```

```python
import functools
import math

import jax
import jax.numpy as jnp
from jax import lax
from jax.experimental import pallas as pl
from jax.experimental.pallas import tpu as pltpu
from jax.sharding import PartitionSpec as P

root_half = 0.7071067811865476
inv_root_two_pi = 0.3989422804014327
LANES = 128
MESH = pl.DeviceIdType.MESH


def gelu_slope(inputs):
    normal_cdf = 0.5 * (1.0 + lax.erf(inputs * root_half))
    return normal_cdf + inputs * inv_root_two_pi * jnp.exp(-0.5 * inputs * inputs)


def signs_of(left, right):
    odd = jnp.bitwise_and(lax.population_count(jnp.bitwise_and(left, right)), 1)
    return (1 - 2 * odd).astype(jnp.float32)


def low_part(hidden_part):
    return hidden_part & -hidden_part


def plain_body(acts, out_grad, w_in, bias_in, w_out, sign_bits, picks):
    images, tokens, width_part = acts.shape
    hidden_part = w_in.shape[1]
    low_len = low_part(hidden_part)
    act_all = lax.all_gather(acts, "rows", axis=2, tiled=True)
    grad_all = lax.all_gather(out_grad, "rows", axis=2, tiled=True)
    pre_act = jnp.einsum("itd,df->itf", act_all, w_in, preferred_element_type=jnp.float32)
    pre_act = pre_act + bias_in.astype(jnp.float32)
    back = jnp.einsum("itd,fd->itf", grad_all, w_out, preferred_element_type=jnp.float32)
    pre_grad = (back * gelu_slope(pre_act)).astype(jnp.bfloat16)
    weight_grad = jnp.einsum("itd,itf->idf", acts, pre_grad, preferred_element_type=jnp.float32)
    local_len = sign_bits.shape[0]
    used = width_part * hidden_part
    flips = (1 - 2 * sign_bits[:used]).astype(jnp.float32)
    signed = (weight_grad.reshape(images, used) * flips).astype(jnp.bfloat16)
    signed = signed.reshape(images, used // low_len, low_len)
    inside = picks % local_len
    high_signs = signs_of((inside // low_len)[:, None], jnp.arange(used // low_len)[None, :])
    low_signs = signs_of((inside % low_len)[:, None], jnp.arange(low_len)[None, :])
    half = jnp.einsum(
        "mq,iql->iml", high_signs.astype(jnp.bfloat16), signed, preferred_element_type=jnp.float32
    )
    shards = lax.axis_size(("cols", "rows"))
    me = lax.axis_index(("cols", "rows"))
    contrib = jnp.sum(half * low_signs[None], axis=2) * signs_of(picks // local_len, me)[None, :]
    return lax.psum(contrib, ("cols", "rows")) * (1.0 / math.sqrt(local_len * shards))


def kernel(
    local_len,
    col_shards,
    acts_hbm,
    grads_hbm,
    w_in_hbm,
    bias_ref,
    w_out_hbm,
    bits_hbm,
    picks_ref,
    out_ref,
    raw,
    blocks,
    w_in,
    w_out,
    bits,
    high,
    low,
    signed,
    pre_sum,
    back_sum,
    mixed,
    row_slots,
    col_slots,
    load_sems,
    twin_sems,
    far_sems,
    layer_sems,
    pass_far_sems,
    pass_layer_sems,
    row_sems,
    col_sems,
):
    images, tokens, width = acts_hbm.shape
    image_rows = blocks.shape[1] // images
    hidden = w_in.shape[1]
    low_len = low.shape[1]
    groups = hidden // low_len
    row_shards = 4
    row = lax.axis_index("rows")
    col = lax.axis_index("cols")
    me_all = col * row_shards + row

    twin = row + 1 - 2 * lax.rem(row, 2)
    far = lax.rem(row + 2, row_shards)
    layer = {"cols": col + 1 - 2 * lax.rem(col, 2)}
    row_peers = [{"rows": lax.rem(row + ahead, row_shards)} for ahead in range(1, row_shards)]
    col_peers = [{"cols": lax.rem(col + ahead, col_shards)} for ahead in range(1, col_shards)]

    barrier = pltpu.get_barrier_semaphore()
    for peer in row_peers + col_peers:
        pl.semaphore_signal(barrier, inc=1, device_id=peer, device_id_type=MESH)

    raw_loads = [
        pltpu.make_async_copy(acts_hbm, raw.at[0], load_sems.at[3]),
        pltpu.make_async_copy(grads_hbm, raw.at[1], load_sems.at[4]),
    ]
    loads = [
        pltpu.make_async_copy(bits_hbm.at[pl.ds(0, bits.shape[0])], bits, load_sems.at[0]),
        pltpu.make_async_copy(w_in_hbm, w_in, load_sems.at[1]),
        pltpu.make_async_copy(w_out_hbm, w_out, load_sems.at[2]),
    ]
    for load in raw_loads + loads[1:] + loads[:1]:
        load.start()
    for load in raw_loads:
        load.wait()

    own_cols = pl.ds(pl.multiple_of(row * width, LANES), width)
    gap = jnp.zeros((image_rows - tokens, width), jnp.bfloat16)
    for image in range(images):
        for kind in range(2):
            blocks[kind, image * image_rows : (image + 1) * image_rows, own_cols] = (
                jnp.concatenate([raw[kind, image], gap], axis=0)
            )
    pl.semaphore_wait(barrier, len(row_peers) + len(col_peers))

    tiles = image_rows // 16
    count = far_sems.shape[1]
    per_image = count // images
    edges = [
        image * image_rows + 16 * (tiles * part // per_image)
        for image in range(images)
        for part in range(per_image)
    ] + [images * image_rows]

    def place(kind, owner, part):
        rows = pl.ds(0, images * image_rows)
        if part is not None:
            rows = pl.ds(edges[part], edges[part + 1] - edges[part])
        return blocks.at[kind, rows, pl.ds(pl.multiple_of(owner * width, LANES), width)]

    def send(ref, sems, at, partner):
        return pltpu.make_async_remote_copy(
            src_ref=ref,
            dst_ref=ref,
            send_sem=sems.at[0, at],
            recv_sem=sems.at[1, at],
            device_id=partner,
            device_id_type=MESH,
        )

    mine = lax.rem(col, 2)
    to_far = [send(place(mine, row, part), far_sems, part, {"rows": far}) for part in range(count)]
    to_twin = [send(place(kind, row, None), twin_sems, kind, {"rows": twin}) for kind in range(2)]
    to_layer = [send(place(mine, far, part), layer_sems, part, layer) for part in range(count)]
    pass_far = [
        send(place(mine, far, part), pass_far_sems, part, {"rows": twin}) for part in range(count)
    ]
    pass_layer = [
        send(place(1 - mine, far, part), pass_layer_sems, part, {"rows": twin})
        for part in range(count)
    ]
    for copy in to_far + to_twin:
        copy.start()

    def relay_far(part):
        to_far[part].wait_recv()
        to_layer[part].start()
        pass_far[part].start()

    def relay_layer(part):
        to_layer[part].wait_recv()
        pass_layer[part].start()

    lane = lax.broadcasted_iota(jnp.int32, (LANES, LANES), 1)

    def make_signs(at, _):
        column = jnp.broadcast_to(picks_ref[pl.ds(at, 1), :], (LANES, LANES)).T
        inside = jnp.bitwise_and(column, local_len - 1)
        upper = jnp.right_shift(inside, low_len.bit_length() - 1)
        lower = jnp.bitwise_and(inside, low_len - 1)
        rows = pl.ds(pl.multiple_of(at * LANES, LANES), LANES)
        for group in range(groups):
            for tile in range(width // LANES):
                spot = groups * (lane + tile * LANES) + group
                start = group * width + tile * LANES
                high[rows, start : start + LANES] = signs_of(upper, spot).astype(jnp.bfloat16)
        for tile in range(low_len // LANES):
            low[rows, tile * LANES : (tile + 1) * LANES] = signs_of(
                lower, lane + tile * LANES
            ).astype(jnp.bfloat16)
        return 0

    def signs(part):
        every = picks_ref.shape[0]
        lax.fori_loop(every * part // 8, every * (part + 1) // 8, make_signs, 0)

    pair = 2 * width

    every_row = slice(0, images * image_rows)

    def products(rows, half, group):
        cols = slice(group * low_len, (group + 1) * low_len)
        part = pl.ds(pl.multiple_of(half * pair, LANES), pair)
        pre = jnp.dot(blocks[0, rows, part], w_in[part, cols], preferred_element_type=jnp.float32)
        back = lax.dot_general(
            blocks[1, rows, part],
            w_out[cols, part],
            (((1,), (1,)), ((), ())),
            preferred_element_type=jnp.float32,
        )
        return pre, back

    here = row // 2

    def own_products(group):
        cols = slice(group * low_len, (group + 1) * low_len)
        pre, back = products(every_row, here, group)
        pre_sum[:, cols] = pre + bias_ref[:, cols].astype(jnp.float32)
        back_sum[:, cols] = back

    def image_signed(image):
        rows = slice(image * image_rows, (image + 1) * image_rows)
        for group in range(groups):
            cols = slice(group * low_len, (group + 1) * low_len)
            pre, back = products(rows, 1 - here, group)
            pre = pre + pre_sum[rows, cols]
            back = back + back_sum[rows, cols]
            pre_grad = (back * gelu_slope(pre)).astype(jnp.bfloat16)
            grad = lax.dot_general(
                blocks[0, rows, own_cols],
                pre_grad,
                (((0,), (0,)), ((), ())),
                preferred_element_type=jnp.float32,
            )
            for tile in range(low_len // LANES):
                first = group * (low_len // LANES) + tile
                flips = bits[pl.ds(first, width, stride=hidden // LANES), :]
                piece = grad[:, tile * LANES : (tile + 1) * LANES]
                signed[
                    image,
                    group * width : (group + 1) * width,
                    tile * LANES : (tile + 1) * LANES,
                ] = (piece * (1 - 2 * flips).astype(jnp.float32)).astype(jnp.bfloat16)

    scale = 1.0 / math.sqrt(local_len * col_shards * row_shards)
    step = 512
    halves = 2
    unit_rows = picks_ref.shape[0] // halves

    def select(image, half):
        def one(at, _):
            rows = pl.ds(pl.multiple_of(at * step, step), step)
            weight = low[rows, :].astype(jnp.float32)
            found = jnp.dot(high[rows, :], signed[image], preferred_element_type=jnp.float32)
            total = jnp.zeros((step, LANES), jnp.float32)
            for tile in range(low_len // LANES):
                cols = slice(tile * LANES, (tile + 1) * LANES)
                total = total + found[:, cols] * weight[:, cols]
            for part in range(step // LANES):
                block = total[part * LANES : (part + 1) * LANES].T
                mixed[image, pl.ds(at * (step // LANES) + part, 1), :] = jnp.sum(
                    block, axis=0, keepdims=True
                )
            return 0

        steps = unit_rows * LANES // step
        lax.fori_loop(half * steps, (half + 1) * steps, one, 0)
        rows = slice(half * unit_rows, (half + 1) * unit_rows)
        owner = jnp.right_shift(picks_ref[rows, :], local_len.bit_length() - 1)
        facing = signs_of(owner, jnp.broadcast_to(me_all, owner.shape)) * scale
        return mixed[image, rows, :] * facing

    def exchange(slots, sems, unit, me, peers):
        return [
            pltpu.make_async_remote_copy(
                src_ref=slots.at[unit, me],
                dst_ref=slots.at[unit, me],
                send_sem=sems.at[0, unit, at],
                recv_sem=sems.at[1, unit, at],
                device_id=peer,
                device_id_type=MESH,
            )
            for at, peer in enumerate(peers)
        ]

    def landed(slots, unit):
        total = slots[unit, 0]
        for at in range(1, slots.shape[1]):
            total = total + slots[unit, at]
        return total

    units = images * halves
    by_row = [exchange(row_slots, row_sems, unit, row, row_peers) for unit in range(units)]
    by_col = [exchange(col_slots, col_sems, unit, col, col_peers) for unit in range(units)]

    def sum_rows(unit, value):
        row_slots[unit, row] = value
        for copy in by_row[unit]:
            copy.start()

    def sum_cols(unit):
        for copy in by_row[unit]:
            copy.wait_recv()
        col_slots[unit, col] = landed(row_slots, unit)
        for copy in by_col[unit]:
            copy.start()

    def finish(unit):
        for copy in by_col[unit]:
            copy.wait_recv()
        image, half = divmod(unit, halves)
        out_ref[image, half * unit_rows : (half + 1) * unit_rows, :] = landed(col_slots, unit)

    signs(0)
    signs(1)
    signs(2)
    relay_far(0)
    signs(3)
    relay_far(1)
    signs(4)
    for load in loads[1:]:
        load.wait()
    for copy in to_twin:
        copy.wait_recv()
    own_products(0)
    relay_far(2)
    relay_layer(0)
    signs(5)
    signs(6)
    relay_layer(1)
    relay_far(3)
    own_products(1)
    relay_layer(2)
    own_products(2)
    relay_far(4)
    signs(7)
    loads[0].wait()
    for copy in pass_far[:per_image] + pass_layer[:per_image]:
        copy.wait_recv()
    relay_layer(3)
    image_signed(0)
    relay_far(5)
    relay_layer(4)
    value = select(0, 0)
    relay_layer(5)
    sum_rows(0, value)
    value = select(0, 1)
    sum_cols(0)
    sum_rows(1, value)
    for copy in pass_far[per_image:] + pass_layer[per_image:]:
        copy.wait_recv()
    image_signed(1)
    finish(0)
    sum_cols(1)
    value = select(1, 0)
    finish(1)
    sum_rows(2, value)
    value = select(1, 1)
    sum_rows(3, value)
    sum_cols(2)
    sum_cols(3)
    finish(2)
    finish(3)
    for copy in to_far + to_twin + to_layer + pass_far + pass_layer:
        copy.wait_send()
    for unit in range(units):
        for copy in by_row[unit] + by_col[unit]:
            copy.wait_send()


def body(acts, out_grad, w_in, bias_in, w_out, sign_bits, picks):
    images, tokens, width = acts.shape
    hidden = w_in.shape[1]
    low_len = low_part(hidden)
    row_shards = lax.axis_size("rows")
    col_shards = lax.axis_size("cols")
    fits = low_len % LANES == 0 and width % LANES == 0 and picks.shape[0] % (16 * LANES) == 0
    if not fits or row_shards != 4 or col_shards % 2 or images != 2 or hidden != 3 * low_len:
        return plain_body(acts, out_grad, w_in, bias_in, w_out, sign_bits, picks)
    local_len = sign_bits.shape[0]
    padded = -(-tokens // 16) * 16
    groups = hidden // low_len
    count = picks.shape[0]
    parts = 6
    halves = 2
    units = images * halves
    slot = (count // LANES // halves, LANES)
    sketch_shape = (images, count // LANES, LANES)
    vmem = pl.BlockSpec(memory_space=pltpu.VMEM)
    anywhere = pl.BlockSpec(memory_space=pl.ANY)
    sketch = pl.pallas_call(
        functools.partial(kernel, local_len, col_shards),
        out_shape=jax.ShapeDtypeStruct(sketch_shape, jnp.float32),
        in_specs=[anywhere, anywhere, anywhere, vmem, anywhere, anywhere, vmem],
        out_specs=vmem,
        scratch_shapes=[
            pltpu.VMEM((2,) + acts.shape, jnp.bfloat16),
            pltpu.VMEM((2, images * padded, row_shards * width), jnp.bfloat16),
            pltpu.VMEM(w_in.shape, jnp.bfloat16),
            pltpu.VMEM(w_out.shape, jnp.bfloat16),
            pltpu.VMEM((width * hidden // LANES, LANES), jnp.int32),
            pltpu.VMEM((count, groups * width), jnp.bfloat16),
            pltpu.VMEM((count, low_len), jnp.bfloat16),
            pltpu.VMEM((images, groups * width, low_len), jnp.bfloat16),
            pltpu.VMEM((images * padded, hidden), jnp.float32),
            pltpu.VMEM((images * padded, hidden), jnp.float32),
            pltpu.VMEM(sketch_shape, jnp.float32),
            pltpu.VMEM((units, row_shards) + slot, jnp.float32),
            pltpu.VMEM((units, col_shards) + slot, jnp.float32),
            pltpu.SemaphoreType.DMA((5,)),
            pltpu.SemaphoreType.DMA((2, 2)),
            pltpu.SemaphoreType.DMA((2, parts)),
            pltpu.SemaphoreType.DMA((2, parts)),
            pltpu.SemaphoreType.DMA((2, parts)),
            pltpu.SemaphoreType.DMA((2, parts)),
            pltpu.SemaphoreType.DMA((2, units, row_shards - 1)),
            pltpu.SemaphoreType.DMA((2, units, col_shards - 1)),
        ],
        compiler_params=pltpu.CompilerParams(
            vmem_limit_bytes=56 * 2**20, collective_id=0, has_side_effects=True
        ),
    )(
        acts,
        out_grad,
        w_in,
        bias_in.reshape(1, hidden),
        w_out,
        sign_bits.reshape(local_len // LANES, LANES),
        picks.reshape(count // LANES, LANES),
    )
    return sketch.reshape(images, count)


def solution(mesh):
    return jax.shard_map(
        body,
        mesh=mesh,
        in_specs=(
            P("groups", None, "rows"),
            P("groups", None, "rows"),
            P(None, "cols"),
            P("cols"),
            P("cols", None),
            P(("cols", "rows")),
            P(),
        ),
        out_specs=P("groups", None),
        check_vma=False,
    )
```

```python
import functools
import math

import jax
import jax.numpy as jnp
from jax import lax
from jax.experimental import pallas as pl
from jax.experimental.pallas import tpu as pltpu
from jax.sharding import PartitionSpec as P

root_half = 0.7071067811865476
inv_root_two_pi = 0.3989422804014327
LANES = 128
MESH = pl.DeviceIdType.MESH


def gelu_slope(inputs):
    normal_cdf = 0.5 * (1.0 + lax.erf(inputs * root_half))
    return normal_cdf + inputs * inv_root_two_pi * jnp.exp(-0.5 * inputs * inputs)


def signs_of(left, right):
    odd = jnp.bitwise_and(lax.population_count(jnp.bitwise_and(left, right)), 1)
    return (1 - 2 * odd).astype(jnp.float32)


def low_part(hidden_part):
    return hidden_part & -hidden_part


def plain_body(acts, out_grad, w_in, bias_in, w_out, sign_bits, picks):
    images, tokens, width_part = acts.shape
    hidden_part = w_in.shape[1]
    low_len = low_part(hidden_part)
    act_all = lax.all_gather(acts, "rows", axis=2, tiled=True)
    grad_all = lax.all_gather(out_grad, "rows", axis=2, tiled=True)
    pre_act = jnp.einsum("itd,df->itf", act_all, w_in, preferred_element_type=jnp.float32)
    pre_act = pre_act + bias_in.astype(jnp.float32)
    back = jnp.einsum("itd,fd->itf", grad_all, w_out, preferred_element_type=jnp.float32)
    pre_grad = (back * gelu_slope(pre_act)).astype(jnp.bfloat16)
    weight_grad = jnp.einsum("itd,itf->idf", acts, pre_grad, preferred_element_type=jnp.float32)
    local_len = sign_bits.shape[0]
    used = width_part * hidden_part
    flips = (1 - 2 * sign_bits[:used]).astype(jnp.float32)
    signed = (weight_grad.reshape(images, used) * flips).astype(jnp.bfloat16)
    signed = signed.reshape(images, used // low_len, low_len)
    inside = picks % local_len
    high_signs = signs_of((inside // low_len)[:, None], jnp.arange(used // low_len)[None, :])
    low_signs = signs_of((inside % low_len)[:, None], jnp.arange(low_len)[None, :])
    half = jnp.einsum(
        "mq,iql->iml", high_signs.astype(jnp.bfloat16), signed, preferred_element_type=jnp.float32
    )
    shards = lax.axis_size(("cols", "rows"))
    me = lax.axis_index(("cols", "rows"))
    contrib = jnp.sum(half * low_signs[None], axis=2) * signs_of(picks // local_len, me)[None, :]
    return lax.psum(contrib, ("cols", "rows")) * (1.0 / math.sqrt(local_len * shards))


def kernel(
    local_len,
    col_shards,
    acts_hbm,
    grads_hbm,
    w_in_hbm,
    bias_ref,
    w_out_hbm,
    bits_hbm,
    picks_ref,
    out_ref,
    raw,
    blocks,
    w_in,
    w_out,
    bits,
    high,
    low,
    signed,
    pre_sum,
    back_sum,
    mixed,
    row_slots,
    col_slots,
    load_sems,
    twin_sems,
    far_sems,
    layer_sems,
    pass_far_sems,
    pass_layer_sems,
    row_sems,
    col_sems,
):
    tokens, images, width = acts_hbm.shape
    image_rows = blocks.shape[1] // images
    hidden = w_in.shape[1]
    low_len = low.shape[1]
    groups = hidden // low_len
    row_shards = 4
    row = lax.axis_index("rows")
    col = lax.axis_index("cols")
    me_all = col * row_shards + row

    twin = row + 1 - 2 * lax.rem(row, 2)
    far = lax.rem(row + 2, row_shards)
    layer = {"cols": col + 1 - 2 * lax.rem(col, 2)}
    row_peers = [{"rows": lax.rem(row + ahead, row_shards)} for ahead in range(1, row_shards)]
    col_peers = [{"cols": lax.rem(col + ahead, col_shards)} for ahead in range(1, col_shards)]

    barrier = pltpu.get_barrier_semaphore()
    for peer in row_peers + col_peers:
        pl.semaphore_signal(barrier, inc=1, device_id=peer, device_id_type=MESH)

    raw_loads = [
        pltpu.make_async_copy(acts_hbm, raw.at[0], load_sems.at[3]),
        pltpu.make_async_copy(grads_hbm, raw.at[1], load_sems.at[4]),
    ]
    loads = [
        pltpu.make_async_copy(bits_hbm.at[pl.ds(0, bits.shape[0])], bits, load_sems.at[0]),
        pltpu.make_async_copy(w_in_hbm, w_in, load_sems.at[1]),
        pltpu.make_async_copy(w_out_hbm, w_out, load_sems.at[2]),
    ]
    for load in raw_loads + loads[1:] + loads[:1]:
        load.start()
    for load in raw_loads:
        load.wait()

    own_cols = pl.ds(pl.multiple_of(row * width, LANES), width)
    gap = jnp.zeros((image_rows - tokens, width), jnp.bfloat16)
    for image in range(images):
        for kind in range(2):
            blocks[kind, image * image_rows : (image + 1) * image_rows, own_cols] = (
                jnp.concatenate([raw[kind, :, image, :], gap], axis=0)
            )
    pl.semaphore_wait(barrier, len(row_peers) + len(col_peers))

    tiles = image_rows // 16
    count = far_sems.shape[1]
    per_image = count // images
    edges = [
        image * image_rows + 16 * (tiles * part // per_image)
        for image in range(images)
        for part in range(per_image)
    ] + [images * image_rows]

    def place(kind, owner, part):
        rows = pl.ds(0, images * image_rows)
        if part is not None:
            rows = pl.ds(edges[part], edges[part + 1] - edges[part])
        return blocks.at[kind, rows, pl.ds(pl.multiple_of(owner * width, LANES), width)]

    def send(ref, sems, at, partner):
        return pltpu.make_async_remote_copy(
            src_ref=ref,
            dst_ref=ref,
            send_sem=sems.at[0, at],
            recv_sem=sems.at[1, at],
            device_id=partner,
            device_id_type=MESH,
        )

    mine = lax.rem(col, 2)
    to_far = [send(place(mine, row, part), far_sems, part, {"rows": far}) for part in range(count)]
    to_twin = [send(place(kind, row, None), twin_sems, kind, {"rows": twin}) for kind in range(2)]
    to_layer = [send(place(mine, far, part), layer_sems, part, layer) for part in range(count)]
    pass_far = [
        send(place(mine, far, part), pass_far_sems, part, {"rows": twin}) for part in range(count)
    ]
    pass_layer = [
        send(place(1 - mine, far, part), pass_layer_sems, part, {"rows": twin})
        for part in range(count)
    ]
    for copy in to_far + to_twin:
        copy.start()

    def relay_far(part):
        to_far[part].wait_recv()
        to_layer[part].start()
        pass_far[part].start()

    def relay_layer(part):
        to_layer[part].wait_recv()
        pass_layer[part].start()

    lane = lax.broadcasted_iota(jnp.int32, (LANES, LANES), 1)

    def make_signs(at, _):
        column = jnp.broadcast_to(picks_ref[pl.ds(at, 1), :], (LANES, LANES)).T
        inside = jnp.bitwise_and(column, local_len - 1)
        upper = jnp.right_shift(inside, low_len.bit_length() - 1)
        lower = jnp.bitwise_and(inside, low_len - 1)
        rows = pl.ds(pl.multiple_of(at * LANES, LANES), LANES)
        for group in range(groups):
            for tile in range(width // LANES):
                spot = groups * (lane + tile * LANES) + group
                start = group * width + tile * LANES
                high[rows, start : start + LANES] = signs_of(upper, spot).astype(jnp.bfloat16)
        for tile in range(low_len // LANES):
            low[rows, tile * LANES : (tile + 1) * LANES] = signs_of(
                lower, lane + tile * LANES
            ).astype(jnp.bfloat16)
        return 0

    def signs(part):
        every = picks_ref.shape[0]
        lax.fori_loop(every * part // 8, every * (part + 1) // 8, make_signs, 0)

    pair = 2 * width

    every_row = slice(0, images * image_rows)

    def products(rows, half, group):
        cols = slice(group * low_len, (group + 1) * low_len)
        part = pl.ds(pl.multiple_of(half * pair, LANES), pair)
        pre = jnp.dot(blocks[0, rows, part], w_in[part, cols], preferred_element_type=jnp.float32)
        back = lax.dot_general(
            blocks[1, rows, part],
            w_out[cols, part],
            (((1,), (1,)), ((), ())),
            preferred_element_type=jnp.float32,
        )
        return pre, back

    here = row // 2

    def own_products(group):
        cols = slice(group * low_len, (group + 1) * low_len)
        pre, back = products(every_row, here, group)
        offsets = bias_ref[...].astype(jnp.float32)
        for tile in range(low_len // LANES):
            at = group * (low_len // LANES) + tile
            pre_sum[:, at * LANES : (at + 1) * LANES] = (
                pre[:, tile * LANES : (tile + 1) * LANES] + offsets[at : at + 1, :]
            )
        back_sum[:, cols] = back

    def image_signed(image):
        rows = slice(image * image_rows, (image + 1) * image_rows)
        for group in range(groups):
            cols = slice(group * low_len, (group + 1) * low_len)
            pre, back = products(rows, 1 - here, group)
            pre = pre + pre_sum[rows, cols]
            back = back + back_sum[rows, cols]
            pre_grad = (back * gelu_slope(pre)).astype(jnp.bfloat16)
            grad = lax.dot_general(
                blocks[0, rows, own_cols],
                pre_grad,
                (((0,), (0,)), ((), ())),
                preferred_element_type=jnp.float32,
            )
            for tile in range(low_len // LANES):
                first = group * (low_len // LANES) + tile
                flips = bits[pl.ds(first, width, stride=hidden // LANES), :]
                piece = grad[:, tile * LANES : (tile + 1) * LANES]
                signed[
                    image,
                    group * width : (group + 1) * width,
                    tile * LANES : (tile + 1) * LANES,
                ] = (piece * (1 - 2 * flips).astype(jnp.float32)).astype(jnp.bfloat16)

    scale = 1.0 / math.sqrt(local_len * col_shards * row_shards)
    step = 8 * LANES
    halves = 2
    unit_rows = picks_ref.shape[0] // halves

    def select(image, half):
        def one(at, _):
            rows = pl.ds(pl.multiple_of(at * step, step), step)
            weight = low[rows, :].astype(jnp.float32)
            found = jnp.dot(high[rows, :], signed[image], preferred_element_type=jnp.float32)
            total = jnp.zeros((step, LANES), jnp.float32)
            for tile in range(low_len // LANES):
                cols = slice(tile * LANES, (tile + 1) * LANES)
                total = total + found[:, cols] * weight[:, cols]
            for part in range(step // LANES):
                block = total[part * LANES : (part + 1) * LANES].T
                mixed[image, pl.ds(at * (step // LANES) + part, 1), :] = jnp.sum(
                    block, axis=0, keepdims=True
                )
            return 0

        steps = unit_rows * LANES // step
        lax.fori_loop(half * steps, (half + 1) * steps, one, 0)
        rows = slice(half * unit_rows, (half + 1) * unit_rows)
        owner = jnp.right_shift(picks_ref[rows, :], local_len.bit_length() - 1)
        facing = signs_of(owner, jnp.broadcast_to(me_all, owner.shape)) * scale
        return mixed[image, rows, :] * facing

    def exchange(slots, sems, unit, me, peers):
        return [
            pltpu.make_async_remote_copy(
                src_ref=slots.at[unit, me],
                dst_ref=slots.at[unit, me],
                send_sem=sems.at[0, unit, at],
                recv_sem=sems.at[1, unit, at],
                device_id=peer,
                device_id_type=MESH,
            )
            for at, peer in enumerate(peers)
        ]

    def landed(slots, unit):
        total = slots[unit, 0]
        for at in range(1, slots.shape[1]):
            total = total + slots[unit, at]
        return total

    units = images * halves
    by_row = [exchange(row_slots, row_sems, unit, row, row_peers) for unit in range(units)]
    by_col = [exchange(col_slots, col_sems, unit, col, col_peers) for unit in range(units)]

    def sum_rows(unit, value):
        row_slots[unit, row] = value
        for copy in by_row[unit]:
            copy.start()

    def sum_cols(unit):
        for copy in by_row[unit]:
            copy.wait_recv()
        col_slots[unit, col] = landed(row_slots, unit)
        for copy in by_col[unit]:
            copy.start()

    def finish(unit):
        for copy in by_col[unit]:
            copy.wait_recv()
        image, half = divmod(unit, halves)
        out_ref[image, half * unit_rows : (half + 1) * unit_rows, :] = landed(col_slots, unit)

    signs(0)
    signs(1)
    signs(2)
    relay_far(0)
    signs(3)
    relay_far(1)
    signs(4)
    for load in loads[1:]:
        load.wait()
    for copy in to_twin:
        copy.wait_recv()
    own_products(0)
    relay_far(2)
    relay_layer(0)
    signs(5)
    signs(6)
    relay_layer(1)
    relay_far(3)
    own_products(1)
    relay_layer(2)
    own_products(2)
    relay_far(4)
    signs(7)
    loads[0].wait()
    for copy in pass_far[:per_image] + pass_layer[:per_image]:
        copy.wait_recv()
    relay_layer(3)
    image_signed(0)
    relay_far(5)
    relay_layer(4)
    value = select(0, 0)
    relay_layer(5)
    sum_rows(0, value)
    value = select(0, 1)
    sum_cols(0)
    sum_rows(1, value)
    for copy in pass_far[per_image:] + pass_layer[per_image:]:
        copy.wait_recv()
    image_signed(1)
    finish(0)
    sum_cols(1)
    value = select(1, 0)
    finish(1)
    sum_rows(2, value)
    value = select(1, 1)
    sum_rows(3, value)
    sum_cols(2)
    sum_cols(3)
    finish(2)
    finish(3)
    for copy in to_far + to_twin + to_layer + pass_far + pass_layer:
        copy.wait_send()
    for unit in range(units):
        for copy in by_row[unit] + by_col[unit]:
            copy.wait_send()


def body(acts, out_grad, w_in, bias_in, w_out, sign_bits, picks):
    images, tokens, width = acts.shape
    hidden = w_in.shape[1]
    low_len = low_part(hidden)
    row_shards = lax.axis_size("rows")
    col_shards = lax.axis_size("cols")
    fits = low_len % LANES == 0 and width % LANES == 0 and picks.shape[0] % (16 * LANES) == 0
    if not fits or row_shards != 4 or col_shards % 2 or images != 2 or hidden != 3 * low_len:
        return plain_body(acts, out_grad, w_in, bias_in, w_out, sign_bits, picks)
    local_len = sign_bits.shape[0]
    padded = -(-tokens // 16) * 16
    groups = hidden // low_len
    count = picks.shape[0]
    parts = 6
    halves = 2
    units = images * halves
    slot = (count // LANES // halves, LANES)
    sketch_shape = (images, count // LANES, LANES)
    vmem = pl.BlockSpec(memory_space=pltpu.VMEM)
    anywhere = pl.BlockSpec(memory_space=pl.ANY)
    sketch = pl.pallas_call(
        functools.partial(kernel, local_len, col_shards),
        out_shape=jax.ShapeDtypeStruct(sketch_shape, jnp.float32),
        in_specs=[anywhere, anywhere, anywhere, vmem, anywhere, anywhere, vmem],
        out_specs=vmem,
        scratch_shapes=[
            pltpu.VMEM((2, tokens, images, width), jnp.bfloat16),
            pltpu.VMEM((2, images * padded, row_shards * width), jnp.bfloat16),
            pltpu.VMEM(w_in.shape, jnp.bfloat16),
            pltpu.VMEM(w_out.shape, jnp.bfloat16),
            pltpu.VMEM((width * hidden // LANES, LANES), jnp.int32),
            pltpu.VMEM((count, groups * width), jnp.bfloat16),
            pltpu.VMEM((count, low_len), jnp.bfloat16),
            pltpu.VMEM((images, groups * width, low_len), jnp.bfloat16),
            pltpu.VMEM((images * padded, hidden), jnp.float32),
            pltpu.VMEM((images * padded, hidden), jnp.float32),
            pltpu.VMEM(sketch_shape, jnp.float32),
            pltpu.VMEM((units, row_shards) + slot, jnp.float32),
            pltpu.VMEM((units, col_shards) + slot, jnp.float32),
            pltpu.SemaphoreType.DMA((5,)),
            pltpu.SemaphoreType.DMA((2, 2)),
            pltpu.SemaphoreType.DMA((2, parts)),
            pltpu.SemaphoreType.DMA((2, parts)),
            pltpu.SemaphoreType.DMA((2, parts)),
            pltpu.SemaphoreType.DMA((2, parts)),
            pltpu.SemaphoreType.DMA((2, units, row_shards - 1)),
            pltpu.SemaphoreType.DMA((2, units, col_shards - 1)),
        ],
        compiler_params=pltpu.CompilerParams(
            vmem_limit_bytes=56 * 2**20, collective_id=0, has_side_effects=True
        ),
    )(
        acts.transpose(1, 0, 2),
        out_grad.transpose(1, 0, 2),
        w_in,
        bias_in.reshape(hidden // LANES, LANES),
        w_out,
        sign_bits.reshape(local_len // LANES, LANES),
        picks.reshape(count // LANES, LANES),
    )
    return sketch.reshape(images, count)


def solution(mesh):
    return jax.shard_map(
        body,
        mesh=mesh,
        in_specs=(
            P("groups", None, "rows"),
            P("groups", None, "rows"),
            P(None, "cols"),
            P("cols"),
            P("cols", None),
            P(("cols", "rows")),
            P(),
        ),
        out_specs=P("groups", None),
        check_vma=False,
    )
```

```python
import functools
import math

import jax
import jax.numpy as jnp
from jax import lax
from jax.experimental import pallas as pl
from jax.experimental.pallas import tpu as pltpu
from jax.sharding import PartitionSpec as P

root_half = 0.7071067811865476
inv_root_two_pi = 0.3989422804014327
LANES = 128
MESH = pl.DeviceIdType.MESH


def gelu_slope(inputs):
    normal_cdf = 0.5 * (1.0 + lax.erf(inputs * root_half))
    return normal_cdf + inputs * inv_root_two_pi * jnp.exp(-0.5 * inputs * inputs)


def signs_of(left, right):
    odd = jnp.bitwise_and(lax.population_count(jnp.bitwise_and(left, right)), 1)
    return (1 - 2 * odd).astype(jnp.float32)


def low_part(hidden_part):
    return hidden_part & -hidden_part


def plain_body(acts, out_grad, w_in, bias_in, w_out, sign_bits, picks):
    images, tokens, width_part = acts.shape
    hidden_part = w_in.shape[1]
    low_len = low_part(hidden_part)
    act_all = lax.all_gather(acts, "rows", axis=2, tiled=True)
    grad_all = lax.all_gather(out_grad, "rows", axis=2, tiled=True)
    pre_act = jnp.einsum("itd,df->itf", act_all, w_in, preferred_element_type=jnp.float32)
    pre_act = pre_act + bias_in.astype(jnp.float32)
    back = jnp.einsum("itd,fd->itf", grad_all, w_out, preferred_element_type=jnp.float32)
    pre_grad = (back * gelu_slope(pre_act)).astype(jnp.bfloat16)
    weight_grad = jnp.einsum("itd,itf->idf", acts, pre_grad, preferred_element_type=jnp.float32)
    local_len = sign_bits.shape[0]
    used = width_part * hidden_part
    flips = (1 - 2 * sign_bits[:used]).astype(jnp.float32)
    signed = (weight_grad.reshape(images, used) * flips).astype(jnp.bfloat16)
    signed = signed.reshape(images, used // low_len, low_len)
    inside = picks % local_len
    high_signs = signs_of((inside // low_len)[:, None], jnp.arange(used // low_len)[None, :])
    low_signs = signs_of((inside % low_len)[:, None], jnp.arange(low_len)[None, :])
    half = jnp.einsum(
        "mq,iql->iml", high_signs.astype(jnp.bfloat16), signed, preferred_element_type=jnp.float32
    )
    shards = lax.axis_size(("cols", "rows"))
    me = lax.axis_index(("cols", "rows"))
    contrib = jnp.sum(half * low_signs[None], axis=2) * signs_of(picks // local_len, me)[None, :]
    return lax.psum(contrib, ("cols", "rows")) * (1.0 / math.sqrt(local_len * shards))


def kernel(
    local_len,
    col_shards,
    acts_hbm,
    grads_hbm,
    w_in_hbm,
    bias_ref,
    w_out_hbm,
    bits_hbm,
    picks_ref,
    out_ref,
    raw,
    blocks,
    w_in,
    w_out,
    bits,
    high,
    low,
    signed,
    pre_sum,
    back_sum,
    mixed,
    row_slots,
    col_slots,
    load_sems,
    twin_sems,
    far_sems,
    layer_sems,
    pass_far_sems,
    pass_layer_sems,
    row_sems,
    col_sems,
):
    tokens, images, width = acts_hbm.shape
    image_rows = blocks.shape[1] // images
    hidden = w_in.shape[1]
    low_len = low.shape[1]
    groups = hidden // low_len
    row_shards = 4
    row = lax.axis_index("rows")
    col = lax.axis_index("cols")
    me_all = col * row_shards + row

    twin = row + 1 - 2 * lax.rem(row, 2)
    far = lax.rem(row + 2, row_shards)
    layer = {"cols": col + 1 - 2 * lax.rem(col, 2)}
    row_peers = [{"rows": lax.rem(row + ahead, row_shards)} for ahead in range(1, row_shards)]
    col_peers = [{"cols": lax.rem(col + ahead, col_shards)} for ahead in range(1, col_shards)]

    barrier = pltpu.get_barrier_semaphore()
    for peer in row_peers + col_peers:
        pl.semaphore_signal(barrier, inc=1, device_id=peer, device_id_type=MESH)

    raw_loads = [
        pltpu.make_async_copy(acts_hbm, raw.at[0], load_sems.at[3]),
        pltpu.make_async_copy(grads_hbm, raw.at[1], load_sems.at[4]),
    ]
    loads = [
        pltpu.make_async_copy(bits_hbm.at[pl.ds(0, bits.shape[0])], bits, load_sems.at[0]),
        pltpu.make_async_copy(w_in_hbm, w_in, load_sems.at[1]),
        pltpu.make_async_copy(w_out_hbm, w_out, load_sems.at[2]),
    ]
    for load in raw_loads + loads[1:] + loads[:1]:
        load.start()
    for load in raw_loads:
        load.wait()

    own_cols = pl.ds(pl.multiple_of(row * width, LANES), width)
    gap = jnp.zeros((image_rows - tokens, width), jnp.bfloat16)
    for image in range(images):
        for kind in range(2):
            blocks[kind, image * image_rows : (image + 1) * image_rows, own_cols] = (
                jnp.concatenate([raw[kind, :, image, :], gap], axis=0)
            )
    pl.semaphore_wait(barrier, len(row_peers) + len(col_peers))

    tiles = image_rows // 16
    count = far_sems.shape[1]
    per_image = count // images
    edges = [
        image * image_rows + 16 * (tiles * part // per_image)
        for image in range(images)
        for part in range(per_image)
    ] + [images * image_rows]

    def place(kind, owner, part):
        rows = pl.ds(0, images * image_rows)
        if part is not None:
            rows = pl.ds(edges[part], edges[part + 1] - edges[part])
        return blocks.at[kind, rows, pl.ds(pl.multiple_of(owner * width, LANES), width)]

    def send(ref, sems, at, partner):
        return pltpu.make_async_remote_copy(
            src_ref=ref,
            dst_ref=ref,
            send_sem=sems.at[0, at],
            recv_sem=sems.at[1, at],
            device_id=partner,
            device_id_type=MESH,
        )

    mine = lax.rem(col, 2)
    to_far = [send(place(mine, row, part), far_sems, part, {"rows": far}) for part in range(count)]
    to_twin = [send(place(kind, row, None), twin_sems, kind, {"rows": twin}) for kind in range(2)]
    to_layer = [send(place(mine, far, part), layer_sems, part, layer) for part in range(count)]
    pass_far = [
        send(place(mine, far, part), pass_far_sems, part, {"rows": twin}) for part in range(count)
    ]
    pass_layer = [
        send(place(1 - mine, far, part), pass_layer_sems, part, {"rows": twin})
        for part in range(count)
    ]
    for copy in to_far + to_twin:
        copy.start()

    def relay_far(part):
        to_far[part].wait_recv()
        to_layer[part].start()
        pass_far[part].start()

    def relay_layer(part):
        to_layer[part].wait_recv()
        pass_layer[part].start()

    lane = lax.broadcasted_iota(jnp.int32, (LANES, LANES), 1)

    def make_signs(at, _):
        column = jnp.broadcast_to(picks_ref[pl.ds(at, 1), :], (LANES, LANES)).T
        inside = jnp.bitwise_and(column, local_len - 1)
        upper = jnp.right_shift(inside, low_len.bit_length() - 1)
        lower = jnp.bitwise_and(inside, low_len - 1)
        rows = pl.ds(pl.multiple_of(at * LANES, LANES), LANES)
        for group in range(groups):
            for tile in range(width // LANES):
                spot = groups * (lane + tile * LANES) + group
                start = group * width + tile * LANES
                high[rows, start : start + LANES] = signs_of(upper, spot).astype(jnp.bfloat16)
        for tile in range(low_len // LANES):
            low[rows, tile * LANES : (tile + 1) * LANES] = signs_of(
                lower, lane + tile * LANES
            ).astype(jnp.bfloat16)
        return 0

    def signs(part):
        every = picks_ref.shape[0]
        lax.fori_loop(every * part // 8, every * (part + 1) // 8, make_signs, 0)

    pair = 2 * width

    every_row = slice(0, images * image_rows)

    def products(rows, half, group):
        cols = slice(group * low_len, (group + 1) * low_len)
        part = pl.ds(pl.multiple_of(half * pair, LANES), pair)
        pre = jnp.dot(blocks[0, rows, part], w_in[part, cols], preferred_element_type=jnp.float32)
        back = lax.dot_general(
            blocks[1, rows, part],
            w_out[cols, part],
            (((1,), (1,)), ((), ())),
            preferred_element_type=jnp.float32,
        )
        return pre, back

    here = row // 2

    def own_products(group):
        cols = slice(group * low_len, (group + 1) * low_len)
        pre, back = products(every_row, here, group)
        offsets = bias_ref[...].astype(jnp.float32)
        for tile in range(low_len // LANES):
            at = group * (low_len // LANES) + tile
            pre_sum[:, at * LANES : (at + 1) * LANES] = (
                pre[:, tile * LANES : (tile + 1) * LANES] + offsets[at : at + 1, :]
            )
        back_sum[:, cols] = back

    def image_signed(image, wanted):
        rows = slice(image * image_rows, (image + 1) * image_rows)
        for group in wanted:
            cols = slice(group * low_len, (group + 1) * low_len)
            pre, back = products(rows, 1 - here, group)
            pre = pre + pre_sum[rows, cols]
            back = back + back_sum[rows, cols]
            pre_grad = (back * gelu_slope(pre)).astype(jnp.bfloat16)
            grad = lax.dot_general(
                blocks[0, rows, own_cols],
                pre_grad,
                (((0,), (0,)), ((), ())),
                preferred_element_type=jnp.float32,
            )
            for tile in range(low_len // LANES):
                first = group * (low_len // LANES) + tile
                flips = bits[pl.ds(first, width, stride=hidden // LANES), :]
                piece = grad[:, tile * LANES : (tile + 1) * LANES]
                signed[
                    image,
                    group * width : (group + 1) * width,
                    tile * LANES : (tile + 1) * LANES,
                ] = (piece * (1 - 2 * flips).astype(jnp.float32)).astype(jnp.bfloat16)

    scale = 1.0 / math.sqrt(local_len * col_shards * row_shards)
    step = 8 * LANES
    halves = 2
    unit_rows = picks_ref.shape[0] // halves

    def select(image, half):
        def one(at, _):
            rows = pl.ds(pl.multiple_of(at * step, step), step)
            weight = low[rows, :].astype(jnp.float32)
            found = jnp.dot(high[rows, :], signed[image], preferred_element_type=jnp.float32)
            total = jnp.zeros((step, LANES), jnp.float32)
            for tile in range(low_len // LANES):
                cols = slice(tile * LANES, (tile + 1) * LANES)
                total = total + found[:, cols] * weight[:, cols]
            for part in range(step // LANES):
                block = total[part * LANES : (part + 1) * LANES].T
                mixed[image, pl.ds(at * (step // LANES) + part, 1), :] = jnp.sum(
                    block, axis=0, keepdims=True
                )
            return 0

        steps = unit_rows * LANES // step
        lax.fori_loop(half * steps, (half + 1) * steps, one, 0)
        rows = slice(half * unit_rows, (half + 1) * unit_rows)
        owner = jnp.right_shift(picks_ref[rows, :], local_len.bit_length() - 1)
        facing = signs_of(owner, jnp.broadcast_to(me_all, owner.shape)) * scale
        return mixed[image, rows, :] * facing

    def exchange(slots, sems, unit, me, peers):
        return [
            pltpu.make_async_remote_copy(
                src_ref=slots.at[unit, me],
                dst_ref=slots.at[unit, me],
                send_sem=sems.at[0, unit, at],
                recv_sem=sems.at[1, unit, at],
                device_id=peer,
                device_id_type=MESH,
            )
            for at, peer in enumerate(peers)
        ]

    def landed(slots, unit):
        total = slots[unit, 0]
        for at in range(1, slots.shape[1]):
            total = total + slots[unit, at]
        return total

    units = images * halves
    by_row = [exchange(row_slots, row_sems, unit, row, row_peers) for unit in range(units)]
    by_col = [exchange(col_slots, col_sems, unit, col, col_peers) for unit in range(units)]

    def sum_rows(unit, value):
        row_slots[unit, row] = value
        for copy in by_row[unit]:
            copy.start()

    def sum_cols(unit):
        for copy in by_row[unit]:
            copy.wait_recv()
        col_slots[unit, col] = landed(row_slots, unit)
        for copy in by_col[unit]:
            copy.start()

    def finish(unit):
        for copy in by_col[unit]:
            copy.wait_recv()
        image, half = divmod(unit, halves)
        out_ref[image, half * unit_rows : (half + 1) * unit_rows, :] = landed(col_slots, unit)

    signs(0)
    signs(1)
    signs(2)
    relay_far(0)
    signs(3)
    relay_far(1)
    signs(4)
    for load in loads[1:]:
        load.wait()
    for copy in to_twin:
        copy.wait_recv()
    own_products(0)
    relay_far(2)
    relay_layer(0)
    signs(5)
    signs(6)
    relay_layer(1)
    relay_far(3)
    own_products(1)
    own_products(2)
    signs(7)
    relay_layer(2)
    loads[0].wait()
    for copy in pass_far[:per_image] + pass_layer[:per_image]:
        copy.wait_recv()
    image_signed(0, [0])
    relay_far(4)
    image_signed(0, [1])
    relay_layer(3)
    image_signed(0, [2])
    relay_far(5)
    relay_layer(4)
    value = select(0, 0)
    relay_layer(5)
    sum_rows(0, value)
    value = select(0, 1)
    sum_cols(0)
    sum_rows(1, value)
    for copy in pass_far[per_image:] + pass_layer[per_image:]:
        copy.wait_recv()
    image_signed(1, range(groups))
    finish(0)
    sum_cols(1)
    value = select(1, 0)
    finish(1)
    sum_rows(2, value)
    value = select(1, 1)
    sum_rows(3, value)
    sum_cols(2)
    sum_cols(3)
    finish(2)
    finish(3)
    for copy in to_far + to_twin + to_layer + pass_far + pass_layer:
        copy.wait_send()
    for unit in range(units):
        for copy in by_row[unit] + by_col[unit]:
            copy.wait_send()


def body(acts, out_grad, w_in, bias_in, w_out, sign_bits, picks):
    images, tokens, width = acts.shape
    hidden = w_in.shape[1]
    low_len = low_part(hidden)
    row_shards = lax.axis_size("rows")
    col_shards = lax.axis_size("cols")
    fits = low_len % LANES == 0 and width % LANES == 0 and picks.shape[0] % (16 * LANES) == 0
    if not fits or row_shards != 4 or col_shards % 2 or images != 2 or hidden != 3 * low_len:
        return plain_body(acts, out_grad, w_in, bias_in, w_out, sign_bits, picks)
    local_len = sign_bits.shape[0]
    padded = -(-tokens // 16) * 16
    groups = hidden // low_len
    count = picks.shape[0]
    parts = 6
    halves = 2
    units = images * halves
    slot = (count // LANES // halves, LANES)
    sketch_shape = (images, count // LANES, LANES)
    vmem = pl.BlockSpec(memory_space=pltpu.VMEM)
    anywhere = pl.BlockSpec(memory_space=pl.ANY)
    sketch = pl.pallas_call(
        functools.partial(kernel, local_len, col_shards),
        out_shape=jax.ShapeDtypeStruct(sketch_shape, jnp.float32),
        in_specs=[anywhere, anywhere, anywhere, vmem, anywhere, anywhere, vmem],
        out_specs=vmem,
        scratch_shapes=[
            pltpu.VMEM((2, tokens, images, width), jnp.bfloat16),
            pltpu.VMEM((2, images * padded, row_shards * width), jnp.bfloat16),
            pltpu.VMEM(w_in.shape, jnp.bfloat16),
            pltpu.VMEM(w_out.shape, jnp.bfloat16),
            pltpu.VMEM((width * hidden // LANES, LANES), jnp.int32),
            pltpu.VMEM((count, groups * width), jnp.bfloat16),
            pltpu.VMEM((count, low_len), jnp.bfloat16),
            pltpu.VMEM((images, groups * width, low_len), jnp.bfloat16),
            pltpu.VMEM((images * padded, hidden), jnp.float32),
            pltpu.VMEM((images * padded, hidden), jnp.float32),
            pltpu.VMEM(sketch_shape, jnp.float32),
            pltpu.VMEM((units, row_shards) + slot, jnp.float32),
            pltpu.VMEM((units, col_shards) + slot, jnp.float32),
            pltpu.SemaphoreType.DMA((5,)),
            pltpu.SemaphoreType.DMA((2, 2)),
            pltpu.SemaphoreType.DMA((2, parts)),
            pltpu.SemaphoreType.DMA((2, parts)),
            pltpu.SemaphoreType.DMA((2, parts)),
            pltpu.SemaphoreType.DMA((2, parts)),
            pltpu.SemaphoreType.DMA((2, units, row_shards - 1)),
            pltpu.SemaphoreType.DMA((2, units, col_shards - 1)),
        ],
        compiler_params=pltpu.CompilerParams(
            vmem_limit_bytes=56 * 2**20, collective_id=0, has_side_effects=True
        ),
    )(
        acts.transpose(1, 0, 2),
        out_grad.transpose(1, 0, 2),
        w_in,
        bias_in.reshape(hidden // LANES, LANES),
        w_out,
        sign_bits.reshape(local_len // LANES, LANES),
        picks.reshape(count // LANES, LANES),
    )
    return sketch.reshape(images, count)


def solution(mesh):
    return jax.shard_map(
        body,
        mesh=mesh,
        in_specs=(
            P("groups", None, "rows"),
            P("groups", None, "rows"),
            P(None, "cols"),
            P("cols"),
            P("cols", None),
            P(("cols", "rows")),
            P(),
        ),
        out_specs=P("groups", None),
        check_vma=False,
    )
```
